128 devices in a mesh: seq: 32 (over z, x, core), exp: 4 (over y).
Axes of the slice: x: 4, y: 4, z: 4, core: 2. Of those that a mesh axis runs over, the one named last changes fastest.
Arguments:
- text_rows: bfloat16 [4096, 4096], P('seq', 'exp'), may hold values from -6 to 6
- image_rows: bfloat16 [2048, 4096], P('seq', 'exp'), may hold values from -6 to 6
- image_dest: int32 [2048], P('seq'), may hold values from 0 to 4095, as said below
- norm_gain: float32 [4096], replicated, may hold values from 0.5 to 1.5
- expert_ids: int32 [4096, 8], P('seq'), may hold values from 0 to 63, all different within a row; in each aligned block of 128 rows (0 to 127, 128 to 255, ...) at most 32 rows name the same one
- gate_weights: float32 [4096, 8], P('seq'), may hold values from 0.1 to 1
- w_gate: bfloat16 [64, 4096, 1536], P('seq', None, 'exp'), may hold values from -0.09375 to 0.09375
- w_up: bfloat16 [64, 4096, 1536], P('seq', None, 'exp'), may hold values from -0.09375 to 0.09375
- w_down: bfloat16 [64, 1536, 4096], P('seq', 'exp'), may hold values from -0.15625 to 0.15625
Outputs:
- block_out: bfloat16 [4096, 4096], P('seq', 'exp')
The draws below stay inside these ranges and needn't reach their ends.
Inputs may be any that keep to these rules, and one draw needn't show every extreme that they name: `image_dest`: all positions are distinct. The 64 rows of one index of seq go to consecutive positions (modulo 4096) that meet at most two blocks of 128 tokens; in every draw some block receives all 64 rows of one index. `expert_ids`: each row names 8 different experts; in each aligned block of 128 rows (the tokens of one index of seq) no expert is named by more than 32 rows, and in some block one expert is named by exactly 32.
All inputs are finite; a program needn't handle non-finite values.
Results may differ from the reference program's by a relative error of at most 0.015.
Values may be sent and summed in bfloat16 or wider, within the bound.
A program may use at most 192 MiB of HBM per device.

```python
import math
import jax
import jax.numpy as jnp
import numpy as np
from jax import lax

D = 4096
FF = 1536
TOP = 8
TOK_DEV = 128
EXPERTS = 64
TOKENS = 4096
IMG_DEV = 64
IMG_ROWS = 2048
CAP = 32
N_SEQ = 32


def draw_image_dest(key, part):
    key = jax.random.fold_in(key, 11)
    first, second = jax.random.split(key)
    places = jax.random.permutation(first, N_SEQ).astype(jnp.int32)
    offsets = jax.random.randint(second, (N_SEQ,), 0, TOK_DEV - IMG_DEV + 1).astype(jnp.int32)
    offsets = jnp.where(places == 0, 0, offsets)
    within = jnp.arange(IMG_DEV, dtype=jnp.int32)
    spots = places[:, None] * TOK_DEV + TOK_DEV // 2 + offsets[:, None] + within[None, :]
    return (spots % TOKENS).reshape(-1).astype(jnp.int32)


def levels(key, dims, cuts, low, largest):
    level, own = 1.0, jax.random.fold_in(key, 6)
    for dim, shards_of in cuts:
        steps = jnp.exp(jax.random.uniform(jax.random.fold_in(own, dim), (shards_of,), jnp.float32, low / len(cuts), largest / len(cuts)))
        level = level * jnp.repeat(steps, dims[dim] // shards_of).reshape([-1 if axis == dim else 1 for axis in range(len(dims))])
    return level


def shared_out(key, own, number, rows, count, top, limit, skew):
    order = jax.random.permutation(key, count)
    crowded, ordinary = load_shares(count, rows * top, limit, skew, True), load_shares(count, rows * top, limit, skew, False)
    places = jnp.arange(count)

    def named(tallies, turn):
        used = int((tallies > 0).sum())
        fixed = max(1, used // 4)
        moved = fixed + (places - fixed + turn * (used - fixed)) % max(1, count - fixed)
        return jnp.zeros((count,), jnp.int32).at[order[jnp.where(places < fixed, places, moved)]].set(jnp.asarray(tallies, jnp.int32))

    tallies = jnp.where(number % 4 == 0, named(crowded, number // 4), named(ordinary, number - number // 4 - 1))
    mixed = jax.random.permutation(jax.random.fold_in(own, 3), count)
    giver, taker = mixed[0:count // 2 * 2:2], mixed[1:count // 2 * 2:2]
    margin = jnp.minimum(tallies[giver] - 1, limit - tallies[taker]) // 2
    margin = jnp.where((giver == order[0]) | (taker == order[0]) | (tallies[taker] == 0), 0, jnp.maximum(margin, 0))
    moved = jax.random.randint(jax.random.fold_in(own, 4), (count // 2,), 0, 1 << 20) % (margin + 1)
    tallies = tallies.at[giver].add(-moved).at[taker].add(moved)
    members = jnp.searchsorted(jnp.cumsum(tallies), jnp.arange(rows * top), side="right").astype(jnp.int32)
    grid = members.reshape(top, rows).T
    grid = grid[jax.random.permutation(jax.random.fold_in(own, 1), rows)]
    turn = jax.random.randint(jax.random.fold_in(own, 2), (rows, 1), 0, top)
    return jnp.take_along_axis(grid, (jnp.arange(top)[None, :] + turn) % top, axis=1)


def load_shares(number_of, total, limit, slope, full):
    weights = [(1 << 20) // math.isqrt(rank ** slope) + 1 for rank in range(1, number_of + 1)]
    largest = limit if full else min(limit, max(-(-total // number_of), total * weights[0] // sum(weights)))
    least = 1 if total - largest >= number_of - 1 else 0
    holding, surplus = [largest] + [least] * (number_of - 1), total - largest - least * (number_of - 1)
    while surplus > 0:
        free = [i for i in range(1, number_of) if holding[i] < largest] or [i for i in range(1, number_of) if holding[i] < limit]
        whole, budget = sum([weights[i] for i in free]), surplus
        for i in free:
            more = min(limit - holding[i], max(1, budget * weights[i] // whole), surplus)
            holding[i] = holding[i] + more
            surplus = surplus - more
    return np.array(holding)


def noise(stream_key, shape, scale, reach, cuts=(), held_as=jnp.bfloat16):
    drawn = scale * jax.random.normal(stream_key, shape, jnp.float32)
    if cuts:
        drawn = drawn * levels(stream_key, shape, cuts, -0.22, 0.18)
    return jnp.clip(drawn, -reach, reach).astype(held_as)


def setup_inputs(seed: int = 0) -> dict:
    key_of = jax.random.split(jax.random.key(seed), 10)
    text_rows = noise(key_of[0], (TOKENS, D), 1.0, 6.0, ((0, 32), (1, 4)))
    image_rows = noise(key_of[1], (IMG_ROWS, D), 1.0, 6.0, ((0, 32), (1, 4)))
    image_dest = draw_image_dest(jax.random.fold_in(key_of[9], 71), 0)
    norm_gain = jnp.clip(1.0 + 0.1 * jax.random.normal(key_of[3], (D,), jnp.float32), 0.5, 1.5)
    expert_ids_keys = jax.random.split(jax.random.fold_in(key_of[4], 1), TOKENS // TOK_DEV)
    expert_ids_turns = jax.random.permutation(jax.random.fold_in(key_of[4], 3), TOKENS // TOK_DEV)
    expert_ids = jax.vmap(lambda own, number: shared_out(jax.random.fold_in(key_of[4], 2), own, number, TOK_DEV, EXPERTS, TOP, CAP, 2))(expert_ids_keys, expert_ids_turns).reshape((TOKENS, TOP))
    gate_weights = jnp.clip(0.1 + 0.9 * jax.random.uniform(key_of[5], (TOKENS, TOP), jnp.float32) ** levels(key_of[5], (TOKENS, TOP), ((0, 32),), -0.2, 0.2), 0.1, 1.0)
    w_gate = noise(key_of[6], (EXPERTS, D, FF), D ** -0.5, 0.09375, ((0, 32), (2, 4)))
    w_up = noise(key_of[7], (EXPERTS, D, FF), D ** -0.5, 0.09375, ((0, 32), (2, 4)))
    w_down = noise(key_of[8], (EXPERTS, FF, D), FF ** -0.5, 0.15625, ((0, 32), (1, 4)))
    return {"text_rows": text_rows, "image_rows": image_rows, "image_dest": image_dest, "norm_gain": norm_gain, "expert_ids": expert_ids, "gate_weights": gate_weights, "w_gate": w_gate, "w_up": w_up, "w_down": w_down}


def reference(text_rows, image_rows, image_dest, norm_gain, expert_ids, gate_weights, w_gate, w_up, w_down):
    merged = text_rows.at[image_dest].set(image_rows)
    merged_f = merged.astype(jnp.float32)
    scale = lax.rsqrt(lax.optimization_barrier(jnp.mean(merged_f * merged_f, axis=1, keepdims=True)) + 1e-06)
    normed = (merged_f * scale * norm_gain.astype(jnp.float32)).astype(jnp.bfloat16)
    ids = expert_ids.reshape(N_SEQ, TOK_DEV * TOP)
    hot = (ids[:, :, None] == jnp.arange(EXPERTS, dtype=jnp.int32)[None, None, :]).astype(jnp.int32)
    rank = lax.optimization_barrier(jnp.sum(jnp.cumsum(hot, axis=1) * hot, axis=2)) - 1
    blocks = jnp.arange(N_SEQ, dtype=jnp.int32)[:, None]
    slots = (ids * (N_SEQ * CAP) + blocks * CAP + rank).reshape(-1).astype(jnp.int32)
    owners = (jnp.arange(TOKENS * TOP, dtype=jnp.int32) // TOP).astype(jnp.int32)
    slot_token = jnp.full((EXPERTS * N_SEQ * CAP,), TOKENS, jnp.int32).at[slots].set(owners)
    slot_token = slot_token.reshape(EXPERTS, N_SEQ * CAP)
    slot_gate = jnp.zeros((EXPERTS * N_SEQ * CAP,), jnp.float32).at[slots].set(gate_weights.reshape(-1))
    slot_gate = slot_gate.reshape(EXPERTS, N_SEQ * CAP)
    padded = jnp.concatenate([normed, jnp.zeros((1, D), jnp.bfloat16)], axis=0)

    def one_expert(total, item):
        gate_mat, up_mat, down_mat, toks, gates = item
        rows = padded[toks]
        gate_part = jnp.dot(rows, gate_mat, preferred_element_type=jnp.float32)
        up_part = jnp.dot(rows, up_mat, preferred_element_type=jnp.float32)
        hidden = (jax.nn.silu(gate_part) * up_part).astype(jnp.bfloat16)
        result = jnp.dot(hidden, down_mat, preferred_element_type=jnp.float32).astype(jnp.bfloat16)
        return (total.at[toks].add(gates[:, None] * result.astype(jnp.float32)), None)
    start = jnp.zeros((TOKENS + 1, D), jnp.float32)
    total, unused = lax.scan(one_expert, start, (w_gate, w_up, w_down, slot_token, slot_gate))
    return (merged_f + total[:TOKENS]).astype(jnp.bfloat16)
```

```python
import functools

import jax
import jax.numpy as jnp
from jax import lax
from jax.experimental import pallas as pl
from jax.experimental.pallas import tpu as pltpu
from jax.sharding import PartitionSpec as P

MESH = pl.DeviceIdType.MESH
CHUNKS = 4
ROWS = 32
QUARTER = 1024
DIMS = "yzx"
ORDERS = ("xyz", "yzx", "zxy")
WIDTHS = ((384, 384, 256), (384, 256, 384), (256, 384, 384), (384, 384, 256))
UNITS = 4
TILES = 8
TILE = 512


def place():
    s = lax.axis_index("seq")
    return {"z": s // 8, "x": (s // 2) % 4, "y": lax.axis_index("exp")}, s % 2


def device(at, core):
    return ((at["z"] * 4 + at["x"]) * 2 + core, at["y"])


def moved(at, axis, by):
    new = dict(at)
    new[axis] = (at[axis] + by + 4) % 4
    return new


def columns(q, p):
    return pl.ds(sum(WIDTHS[q][:p]), WIDTHS[q][p])


def expert_kernel(
    normed, merged, gates, w_gate, w_up, w_down,
    out, far_gate, far_up, far_down,
    X, H, WB, WD, half1, half2, half3, full1, full2, full3,
    own_sem, wb_sem, wd_sem, far_send, far_recv, ag_send, ag_recv, rs_send, rs_recv,
):
    me, core = place()
    barrier = pltpu.get_barrier_semaphore()
    neighbours = [device(moved(me, a, d), core) for a in "xyz" for d in (1, -1)]
    neighbours.append(device(me, 1 - core))
    for who in neighbours:
        pl.semaphore_signal(barrier, inc=1, device_id=who, device_id_type=MESH)
    pl.semaphore_wait(barrier, len(neighbours))

    def slab(q, full, at, cols, rows=pl.ds(0, ROWS)):
        index = tuple(slice(None) if a in full else at[a] for a in DIMS)
        return (q, *index, rows, cols)

    far = [
        pltpu.make_async_remote_copy(
            src_ref=src, dst_ref=dst, send_sem=far_send.at[i], recv_sem=far_recv.at[i],
            device_id=device(me, 1 - core), device_id_type=MESH,
        )
        for i, (src, dst) in enumerate(
            ((w_gate, far_gate), (w_up, far_up), (w_down, far_down))
        )
    ]
    own = [
        pltpu.make_async_copy(
            normed.at[pl.ds(ROWS * q, ROWS)], X.at[q, me["y"], me["z"], me["x"]], own_sem.at[q]
        )
        for q in range(CHUNKS)
    ]

    def ag_copy(q, p, k, j):
        order = ORDERS[p]
        axis, full = order[k], order[:k]
        way = 1 if j % 2 == 0 else -1
        cols = columns(q, p)
        if j < 2:
            index = slab(q, full, me, cols)
            src = normed.at[pl.ds(ROWS * q, ROWS), cols] if k == 0 else X.at[index]
        else:
            rows = pl.ds(0, 16) if j == 2 else pl.ds(16, 16)
            index = slab(q, full, moved(me, axis, -way), cols, rows)
            src = X.at[index]
        return pltpu.make_async_remote_copy(
            src_ref=src, dst_ref=X.at[index],
            send_sem=ag_send.at[q, p, k, j], recv_sem=ag_recv.at[q, p, k, j],
            device_id=device(moved(me, axis, way), core), device_id_type=MESH,
        )

    def ag_first(q, k):
        for p in range(3):
            if k:
                for j in (2, 3):
                    ag_copy(q, p, k - 1, j).wait_recv()
            for j in (0, 1):
                ag_copy(q, p, k, j).start()

    def ag_second(q, k):
        for p in range(3):
            for j in (0, 1):
                ag_copy(q, p, k, j).wait_recv()
                ag_copy(q, p, k, j + 2).start()

    def ag_end(q):
        for p in range(3):
            for j in (2, 3):
                ag_copy(q, p, 2, j).wait_recv()
            for k in range(3):
                for j in range(4):
                    ag_copy(q, p, k, j).wait_send()

    halves, fulls = (half1, half2, half3), (full1, full2, full3)

    def rs_refs(q, p, k, j):
        order = ORDERS[p][::-1]
        axis, full = order[k], order[k + 1:]
        cols = columns(q, p)
        way = 1 if j % 2 == 0 else -1
        mid = (slice(None),) * len(full)
        if j < 2:
            rows = pl.ds(0, 16) if j == 0 else pl.ds(16, 16)
            sent = slab(q, full, moved(me, axis, 2), cols, rows)
            kept = slab(q, full, moved(me, axis, way), cols, rows)
            got = halves[k].at[(q, j, *mid, slice(None), cols)]
        else:
            sent = slab(q, full, moved(me, axis, way), cols)
            kept = slab(q, full, me, cols)
            got = fulls[k].at[(q, j - 2, *mid, slice(None), cols)]
        return sent, kept, got, device(moved(me, axis, way), core)

    def rs_copy(q, p, k, j):
        sent, _, got, who = rs_refs(q, p, k, j)
        return pltpu.make_async_remote_copy(
            src_ref=X.at[sent], dst_ref=got,
            send_sem=rs_send.at[q, p, k, j], recv_sem=rs_recv.at[q, p, k, j],
            device_id=who, device_id_type=MESH,
        )

    def rs_first(q, k):
        for p in range(3):
            for j in (0, 1):
                rs_copy(q, p, k, j).start()

    def f32(v):
        return v.astype(jnp.float32)

    def rs_second(q, k):
        for p in range(3):
            for j in (0, 1):
                rs_copy(q, p, k, j).wait_recv()
                _, kept, got, _ = rs_refs(q, p, k, j)
                X[kept] = (f32(X[kept]) + f32(got[...])).astype(jnp.bfloat16)
                rs_copy(q, p, k, j + 2).start()

    def rs_end(q, k):
        for p in range(3):
            _, kept, a, _ = rs_refs(q, p, k, 2)
            b = rs_refs(q, p, k, 3)[2]
            for j in (2, 3):
                rs_copy(q, p, k, j).wait_recv()
            total = f32(X[kept]) + f32(a[...]) + f32(b[...])
            if k < 2:
                X[kept] = total.astype(jnp.bfloat16)
                for j in (0, 1):
                    rs_copy(q, p, k + 1, j).start()
            else:
                rows, cols = pl.ds(ROWS * q, ROWS), columns(q, p)
                out[rows, cols] = (total + f32(merged[rows, cols])).astype(jnp.bfloat16)

    def wb_copies(slot, gate, up, e):
        return [
            pltpu.make_async_copy(gate.at[e], WB.at[slot, :, pl.ds(0, 384)], wb_sem.at[slot, 0]),
            pltpu.make_async_copy(up.at[e], WB.at[slot, :, pl.ds(384, 384)], wb_sem.at[slot, 1]),
        ]

    def wb_start(e, slot):
        @pl.when(e < 2)
        def _():
            for c in wb_copies(slot, w_gate, w_up, e):
                c.start()

        @pl.when(e >= 2)
        def _():
            for c in wb_copies(slot, far_gate, far_up, e - 2):
                c.start()

    def wd_copies(n, slot):
        cols = pl.ds(pl.multiple_of(n * TILE, TILE), TILE)
        return [
            pltpu.make_async_copy(w_down.at[:, :, cols], WD.at[slot, pl.ds(0, 2)], wd_sem.at[slot, 0]),
            pltpu.make_async_copy(far_down.at[:, :, cols], WD.at[slot, pl.ds(2, 2)], wd_sem.at[slot, 1]),
        ]

    plan = {
        (0, 0): [lambda: ag_second(1, 2), lambda: ag_first(2, 2)],
        (0, 3): [lambda: ag_second(2, 2), lambda: ag_first(3, 2)],
        (0, 8): [lambda: ag_second(3, 2)],
        (0, 11): [lambda: ag_end(1)],
        (1, 11): [lambda: ag_end(2)],
        (2, 11): [lambda: ag_end(3)],
    }

    def add(q, u, f, *args):
        plan.setdefault((q, u), []).append(lambda: f(*args))

    for q in range(CHUNKS):
        add(q, 11, rs_first, q, 0)
        if q < CHUNKS - 1:
            add(q + 1, 1, rs_second, q, 0)
            add(q + 1, 3, rs_end, q, 0)
            add(q + 1, 5, rs_second, q, 1)
            add(q + 1, 7, rs_end, q, 1)
            add(q + 1, 9, rs_second, q, 2)
            add(q + 1, 10, rs_end, q, 2)

    def hooks(q, u, units):
        for (pq, pu), actions in sorted(plan.items()):
            if pu in units:
                @pl.when((q == pq) & (u == pu))
                def _(actions=actions):
                    for act in actions:
                        act()

    for c in own:
        c.start()
    for q in range(CHUNKS):
        ag_first(q, 0)
    for c in far:
        c.start()
    wb_start(0, 0)
    for c in own:
        c.wait()
    for k in range(2):
        for q in range(CHUNKS):
            ag_second(q, k)
        for q in range(CHUNKS if k == 0 else 2):
            ag_first(q, k + 1)
    ag_second(0, 2)
    ag_end(0)

    def chunk(q, carry):
        def unit(e, carry):
            slot = lax.rem(e, 2)

            @pl.when((q == 0) & (e == 1))
            def _():
                for c in far:
                    c.wait_recv()

            @pl.when((e < UNITS - 1) | (q < CHUNKS - 1))
            def _():
                wb_start(lax.rem(e + 1, UNITS), 1 - slot)

            @pl.when(e == UNITS - 1)
            def _():
                for c in wd_copies(0, 0):
                    c.start()

            for c in wb_copies(slot, w_gate, w_up, 0):
                c.wait()

            def rows(m, carry):
                part = pl.ds(2 * m, 2)
                acc = jnp.zeros((256, 768), jnp.float32)
                for y in range(4):
                    acc += jnp.dot(
                        X[q, y, part].reshape(256, QUARTER),
                        WB[slot, pl.ds(QUARTER * y, QUARTER), :],
                        preferred_element_type=jnp.float32,
                    )
                g, u = acc[:, :384], acc[:, 384:]
                here = pl.ds(pl.multiple_of(256 * m, 256), 256)
                lane = lax.broadcasted_iota(jnp.int32, (256, 128), 1)
                weight = jnp.sum(jnp.where(lane == e, gates[q, here, :], 0.0), axis=1, keepdims=True)
                hidden = g / (1.0 + jnp.exp(-g)) * u * weight
                H[here, pl.ds(pl.multiple_of(e * 384, 128), 384)] = hidden.astype(jnp.bfloat16)
                return carry

            lax.fori_loop(0, 2, rows, 0)
            hooks(q, e, range(UNITS))
            return carry

        lax.fori_loop(0, UNITS, unit, 0)

        def tile(n, carry):
            slot = lax.rem(n, 2)

            @pl.when(n < TILES - 1)
            def _():
                for c in wd_copies(n + 1, 1 - slot):
                    c.start()

            for c in wd_copies(n, slot):
                c.wait()
            acc = jnp.dot(
                H[...], WD[slot].reshape(1536, TILE), preferred_element_type=jnp.float32
            )
            X[q, n // 2, :, :, :, pl.ds(pl.multiple_of(lax.rem(n, 2) * TILE, TILE), TILE)] = (
                acc.astype(jnp.bfloat16).reshape(4, 4, ROWS, TILE)
            )
            hooks(q, n + UNITS, range(UNITS, UNITS + TILES))
            return carry

        lax.fori_loop(0, TILES, tile, 0)
        return carry

    lax.fori_loop(0, CHUNKS, chunk, 0)
    last = CHUNKS - 1
    for k in range(3):
        rs_second(last, k)
        rs_end(last, k)
    for c in far:
        c.wait_send()
    for q in range(CHUNKS):
        for p in range(3):
            for k in range(3):
                for j in range(4):
                    rs_copy(q, p, k, j).wait_send()


def experts(normed, merged, gates, w_gate, w_up, w_down):
    bf = jnp.bfloat16
    hbm = pl.BlockSpec(memory_space=pl.ANY)
    vmem = pl.BlockSpec(memory_space=pltpu.VMEM)
    dma = pltpu.SemaphoreType.DMA
    flops = 2 * 2048 * 1536 * 4096 * 3
    return pl.pallas_call(
        expert_kernel,
        out_shape=[
            jax.ShapeDtypeStruct(merged.shape, bf),
            jax.ShapeDtypeStruct(w_gate.shape, bf),
            jax.ShapeDtypeStruct(w_up.shape, bf),
            jax.ShapeDtypeStruct(w_down.shape, bf),
        ],
        in_specs=[vmem, vmem, vmem, hbm, hbm, hbm],
        out_specs=[vmem, hbm, hbm, hbm],
        scratch_shapes=[
            pltpu.VMEM((CHUNKS, 4, 4, 4, ROWS, QUARTER), bf),
            pltpu.VMEM((512, 1536), bf),
            pltpu.VMEM((2, 4096, 768), bf),
            pltpu.VMEM((2, 4, 384, TILE), bf),
            pltpu.VMEM((CHUNKS, 2, 4, 4, 16, QUARTER), bf),
            pltpu.VMEM((CHUNKS, 2, 4, 16, QUARTER), bf),
            pltpu.VMEM((CHUNKS, 2, 16, QUARTER), bf),
            pltpu.VMEM((CHUNKS, 2, 4, 4, ROWS, QUARTER), bf),
            pltpu.VMEM((CHUNKS, 2, 4, ROWS, QUARTER), bf),
            pltpu.VMEM((CHUNKS, 2, ROWS, QUARTER), bf),
            dma((CHUNKS,)),
            dma((2, 2)),
            dma((2, 2)),
            dma((3,)),
            dma((3,)),
            dma((CHUNKS, 3, 3, 4)),
            dma((CHUNKS, 3, 3, 4)),
            dma((CHUNKS, 3, 3, 4)),
            dma((CHUNKS, 3, 3, 4)),
        ],
        cost_estimate=pl.CostEstimate(
            flops=flops, bytes_accessed=150 << 20, transcendentals=2048 * 1536
        ),
        compiler_params=pltpu.CompilerParams(
            collective_id=0, has_side_effects=True, vmem_limit_bytes=60 << 20
        ),
    )(normed, merged, gates, w_gate, w_up, w_down)[0]


def on_device(
    text_rows, image_rows, image_dest, norm_gain, expert_ids, gate_weights, w_gate, w_up, w_down
):
    seq_count = lax.axis_size("seq")
    tok_dev = text_rows.shape[0]
    s = lax.axis_index("seq")
    y = lax.axis_index("exp")
    rows_all = lax.all_gather(image_rows, "seq").reshape(-1, QUARTER)
    dest_all = lax.all_gather(image_dest, "seq").reshape(1, -1)
    place_hot = (jnp.arange(tok_dev, dtype=jnp.int32) + s * tok_dev)[:, None] == dest_all
    placed = jnp.dot(place_hot.astype(jnp.bfloat16), rows_all, preferred_element_type=jnp.float32)
    present = jnp.any(place_hot, axis=1)
    merged = jnp.where(present[:, None], placed.astype(jnp.bfloat16), text_rows)
    merged_f = merged.astype(jnp.float32)
    squares = lax.psum(jnp.sum(merged_f * merged_f, axis=1, keepdims=True), "exp")
    scale = lax.rsqrt(squares / 4096 + 1e-06)
    gain = lax.dynamic_slice(norm_gain, (y * QUARTER,), (QUARTER,))
    normed = (merged_f * scale * gain).astype(jnp.bfloat16)
    ids = lax.all_gather(expert_ids, "seq").reshape(16, 2, tok_dev, 8)
    weights = lax.all_gather(gate_weights, "seq").reshape(16, 2, tok_dev, 8)
    core = s % 2
    ids = lax.dynamic_index_in_dim(ids, core, 1, keepdims=False)
    weights = lax.dynamic_index_in_dim(weights, core, 1, keepdims=False)
    lane = jnp.arange(128, dtype=jnp.int32)
    chip = s - core
    expert = jnp.where(lane < 4, 2 * chip + (lane + 2 * core) % 4, -1)
    gates = jnp.sum(
        jnp.where(ids[..., None] == expert, weights[..., None], 0.0), axis=2
    )
    gates = gates.reshape(16, CHUNKS, ROWS, 128).transpose(1, 0, 2, 3).reshape(CHUNKS, 512, 128)
    return experts(normed, merged, gates, w_gate, w_up, w_down)


def solution(mesh):
    placed = (
        P("seq", "exp"),
        P("seq", "exp"),
        P("seq"),
        P(),
        P("seq", None),
        P("seq", None),
        P("seq", None, "exp"),
        P("seq", None, "exp"),
        P("seq", "exp", None),
    )
    return jax.shard_map(
        on_device, mesh=mesh, in_specs=placed, out_specs=P("seq", "exp"), check_vma=False
    )
```

```python
import functools

import jax
import jax.numpy as jnp
from jax import lax
from jax.experimental import pallas as pl
from jax.experimental.pallas import tpu as pltpu
from jax.sharding import PartitionSpec as P

MESH = pl.DeviceIdType.MESH
CHUNKS = 4
ROWS = 32
QUARTER = 1024
DIMS = "yzx"
ORDERS = ("xyz", "yzx", "zxy")
WIDTHS = ((384, 384, 256), (384, 256, 384), (256, 384, 384), (384, 384, 256))
UNITS = 4
TILES = 8
TILE = 512


def place():
    s = lax.axis_index("seq")
    return {"z": s // 8, "x": (s // 2) % 4, "y": lax.axis_index("exp")}, s % 2


def device(at, core):
    return ((at["z"] * 4 + at["x"]) * 2 + core, at["y"])


def moved(at, axis, by):
    new = dict(at)
    new[axis] = (at[axis] + by + 4) % 4
    return new


def columns(q, p):
    return pl.ds(sum(WIDTHS[q][:p]), WIDTHS[q][p])


def expert_kernel(
    normed, merged, gates, w_gate, w_up, w_down,
    out, far_gate, far_up, far_down,
    X, H, WB, WD, half1, half2, half3, full1, full2, full3,
    own_sem, wb_sem, wd_sem, far_send, far_recv, ag_send, ag_recv, rs_send, rs_recv,
):
    me, core = place()
    barrier = pltpu.get_barrier_semaphore()
    neighbours = [device(moved(me, a, d), core) for a in "xyz" for d in (1, -1)]
    neighbours.append(device(me, 1 - core))
    for who in neighbours:
        pl.semaphore_signal(barrier, inc=1, device_id=who, device_id_type=MESH)
    pl.semaphore_wait(barrier, len(neighbours))

    def slab(q, full, at, cols, rows=pl.ds(0, ROWS)):
        index = tuple(slice(None) if a in full else at[a] for a in DIMS)
        return (q, *index, rows, cols)

    far = [
        pltpu.make_async_remote_copy(
            src_ref=src, dst_ref=dst, send_sem=far_send.at[i], recv_sem=far_recv.at[i],
            device_id=device(me, 1 - core), device_id_type=MESH,
        )
        for i, (src, dst) in enumerate(
            (
                (w_gate.at[0], far_gate.at[0]),
                (w_up.at[0], far_up.at[0]),
                (w_gate.at[1], far_gate.at[1]),
                (w_up.at[1], far_up.at[1]),
                (w_down, far_down),
            )
        )
    ]
    own = [
        pltpu.make_async_copy(
            normed.at[pl.ds(ROWS * q, ROWS)], X.at[q, me["y"], me["z"], me["x"]], own_sem.at[q]
        )
        for q in range(CHUNKS)
    ]

    def ag_copy(q, p, k, j):
        order = ORDERS[p]
        axis, full = order[k], order[:k]
        way = 1 if j % 2 == 0 else -1
        cols = columns(q, p)
        if j < 2:
            index = slab(q, full, me, cols)
            src = normed.at[pl.ds(ROWS * q, ROWS), cols] if k == 0 else X.at[index]
        else:
            rows = pl.ds(0, 16) if j == 2 else pl.ds(16, 16)
            index = slab(q, full, moved(me, axis, -way), cols, rows)
            src = X.at[index]
        return pltpu.make_async_remote_copy(
            src_ref=src, dst_ref=X.at[index],
            send_sem=ag_send.at[q, p, k, j], recv_sem=ag_recv.at[q, p, k, j],
            device_id=device(moved(me, axis, way), core), device_id_type=MESH,
        )

    def ag_first(q, k):
        for p in range(3):
            if k:
                for j in (2, 3):
                    ag_copy(q, p, k - 1, j).wait_recv()
            for j in (0, 1):
                ag_copy(q, p, k, j).start()

    def ag_second(q, k):
        for p in range(3):
            for j in (0, 1):
                ag_copy(q, p, k, j).wait_recv()
                ag_copy(q, p, k, j + 2).start()

    def ag_end(q):
        for p in range(3):
            for j in (2, 3):
                ag_copy(q, p, 2, j).wait_recv()
            for k in range(3):
                for j in range(4):
                    ag_copy(q, p, k, j).wait_send()

    halves, fulls = (half1, half2, half3), (full1, full2, full3)

    def rs_refs(q, p, k, j):
        order = ORDERS[p][::-1]
        axis, full = order[k], order[k + 1:]
        cols = columns(q, p)
        way = 1 if j % 2 == 0 else -1
        mid = (slice(None),) * len(full)
        if j < 2:
            rows = pl.ds(0, 16) if j == 0 else pl.ds(16, 16)
            sent = slab(q, full, moved(me, axis, 2), cols, rows)
            kept = slab(q, full, moved(me, axis, way), cols, rows)
            got = halves[k].at[(q, j, *mid, slice(None), cols)]
        else:
            sent = slab(q, full, moved(me, axis, way), cols)
            kept = slab(q, full, me, cols)
            got = fulls[k].at[(q, j - 2, *mid, slice(None), cols)]
        return sent, kept, got, device(moved(me, axis, way), core)

    def rs_copy(q, p, k, j):
        sent, _, got, who = rs_refs(q, p, k, j)
        return pltpu.make_async_remote_copy(
            src_ref=X.at[sent], dst_ref=got,
            send_sem=rs_send.at[q, p, k, j], recv_sem=rs_recv.at[q, p, k, j],
            device_id=who, device_id_type=MESH,
        )

    def rs_first(q, k):
        for p in range(3):
            for j in (0, 1):
                rs_copy(q, p, k, j).start()

    def f32(v):
        return v.astype(jnp.float32)

    def rs_second(q, k):
        for p in range(3):
            for j in (0, 1):
                rs_copy(q, p, k, j).wait_recv()
                _, kept, got, _ = rs_refs(q, p, k, j)
                X[kept] = (f32(X[kept]) + f32(got[...])).astype(jnp.bfloat16)
                rs_copy(q, p, k, j + 2).start()

    def rs_end(q, k):
        for p in range(3):
            _, kept, a, _ = rs_refs(q, p, k, 2)
            b = rs_refs(q, p, k, 3)[2]
            for j in (2, 3):
                rs_copy(q, p, k, j).wait_recv()
            total = f32(X[kept]) + f32(a[...]) + f32(b[...])
            if k < 2:
                X[kept] = total.astype(jnp.bfloat16)
                for j in (0, 1):
                    rs_copy(q, p, k + 1, j).start()
            else:
                rows, cols = pl.ds(ROWS * q, ROWS), columns(q, p)
                out[rows, cols] = (total + f32(merged[rows, cols])).astype(jnp.bfloat16)

    def wb_copies(slot, gate, up, e):
        return [
            pltpu.make_async_copy(gate.at[e], WB.at[slot, :, pl.ds(0, 384)], wb_sem.at[slot, 0]),
            pltpu.make_async_copy(up.at[e], WB.at[slot, :, pl.ds(384, 384)], wb_sem.at[slot, 1]),
        ]

    def wb_start(e, slot):
        @pl.when(e < 2)
        def _():
            for c in wb_copies(slot, w_gate, w_up, e):
                c.start()

        @pl.when(e >= 2)
        def _():
            for c in wb_copies(slot, far_gate, far_up, e - 2):
                c.start()

    def wd_copies(n, slot):
        cols = pl.ds(pl.multiple_of(n * TILE, TILE), TILE)
        return [
            pltpu.make_async_copy(w_down.at[:, :, cols], WD.at[slot, pl.ds(0, 2)], wd_sem.at[slot, 0]),
            pltpu.make_async_copy(far_down.at[:, :, cols], WD.at[slot, pl.ds(2, 2)], wd_sem.at[slot, 1]),
        ]

    plan = {
        (0, 0): [lambda: ag_second(1, 2), lambda: ag_first(2, 2)],
        (0, 3): [lambda: ag_second(2, 2), lambda: ag_first(3, 2)],
        (0, 11): [lambda: ag_end(1)],
        (1, 0): [lambda: ag_second(3, 2)],
        (1, 11): [lambda: ag_end(2)],
        (2, 11): [lambda: ag_end(3)],
    }

    def add(q, u, f, *args):
        plan.setdefault((q, u), []).append(lambda: f(*args))

    for q in range(CHUNKS):
        add(q, 11, rs_first, q, 0)
        if q < CHUNKS - 1:
            add(q + 1, 1, rs_second, q, 0)
            add(q + 1, 3, rs_end, q, 0)
            add(q + 1, 6, rs_second, q, 1)
            add(q + 1, 9, rs_end, q, 1)
            add(q + 1, 11, rs_second, q, 2)
            if q < CHUNKS - 2:
                add(q + 2, 0, rs_end, q, 2)

    def hooks(q, u, units):
        for (pq, pu), actions in sorted(plan.items()):
            if pu in units:
                @pl.when((q == pq) & (u == pu))
                def _(actions=actions):
                    for act in actions:
                        act()

    for c in own:
        c.start()
    for q in range(CHUNKS):
        ag_first(q, 0)
    for c in far[:2]:
        c.start()
    wb_start(0, 0)
    for c in own:
        c.wait()
    ag_second(0, 0)
    ag_first(0, 1)
    for q in range(1, CHUNKS):
        ag_second(q, 0)
    for c in far[2:4]:
        c.start()
    ag_second(0, 1)
    ag_first(0, 2)
    for q in range(1, CHUNKS):
        ag_first(q, 1)
    far[4].start()
    for q in range(1, CHUNKS):
        ag_second(q, 1)
    ag_second(0, 2)
    ag_first(1, 2)
    ag_end(0)

    def chunk(q, carry):
        def unit(e, carry):
            slot = lax.rem(e, 2)

            for first, ready in ((1, far[:2]), (2, far[2:4]), (3, far[4:])):
                @pl.when((q == 0) & (e == first))
                def _(ready=ready):
                    for c in ready:
                        c.wait_recv()

            @pl.when((e < UNITS - 1) | (q < CHUNKS - 1))
            def _():
                wb_start(lax.rem(e + 1, UNITS), 1 - slot)

            @pl.when(e == UNITS - 1)
            def _():
                for c in wd_copies(0, 0):
                    c.start()

            for c in wb_copies(slot, w_gate, w_up, 0):
                c.wait()

            acc = jnp.zeros((512, 768), jnp.float32)
            for y in range(4):
                acc += jnp.dot(
                    X[q, y].reshape(512, QUARTER),
                    WB[slot, pl.ds(QUARTER * y, QUARTER), :],
                    preferred_element_type=jnp.float32,
                )
            g, u = acc[:, :384], acc[:, 384:]
            lane = lax.broadcasted_iota(jnp.int32, (16, ROWS, 128), 2)
            block = lax.broadcasted_iota(jnp.int32, (16, ROWS, 128), 0)
            rows = gates[pl.ds(pl.multiple_of(q * ROWS, ROWS), ROWS), :]
            weight = jnp.where(lane == 8 * block + e, rows[None], 0.0).reshape(512, 128)
            weight = jnp.sum(weight, axis=1, keepdims=True)
            hidden = g / (1.0 + jnp.exp(-g)) * u * weight
            H[:, pl.ds(pl.multiple_of(e * 384, 128), 384)] = hidden.astype(jnp.bfloat16)
            hooks(q, e, range(UNITS))
            return carry

        lax.fori_loop(0, UNITS, unit, 0)

        def tile(n, carry):
            slot = lax.rem(n, 2)

            @pl.when(n < TILES - 1)
            def _():
                for c in wd_copies(n + 1, 1 - slot):
                    c.start()

            for c in wd_copies(n, slot):
                c.wait()
            acc = jnp.dot(
                H[...], WD[slot].reshape(1536, TILE), preferred_element_type=jnp.float32
            )
            X[q, n // 2, :, :, :, pl.ds(pl.multiple_of(lax.rem(n, 2) * TILE, TILE), TILE)] = (
                acc.astype(jnp.bfloat16).reshape(4, 4, ROWS, TILE)
            )
            hooks(q, n + UNITS, range(UNITS, UNITS + TILES))
            return carry

        lax.fori_loop(0, TILES, tile, 0)
        return carry

    lax.fori_loop(0, CHUNKS, chunk, 0)
    last = CHUNKS - 1
    rs_end(last - 1, 2)
    for k in range(3):
        rs_second(last, k)
        rs_end(last, k)
    for c in far:
        c.wait_send()
    for q in range(CHUNKS):
        for p in range(3):
            for k in range(3):
                for j in range(4):
                    rs_copy(q, p, k, j).wait_send()


def experts(normed, merged, gates, w_gate, w_up, w_down):
    bf = jnp.bfloat16
    hbm = pl.BlockSpec(memory_space=pl.ANY)
    vmem = pl.BlockSpec(memory_space=pltpu.VMEM)
    dma = pltpu.SemaphoreType.DMA
    flops = 2 * 2048 * 1536 * 4096 * 3
    return pl.pallas_call(
        expert_kernel,
        out_shape=[
            jax.ShapeDtypeStruct(merged.shape, bf),
            jax.ShapeDtypeStruct(w_gate.shape, bf),
            jax.ShapeDtypeStruct(w_up.shape, bf),
            jax.ShapeDtypeStruct(w_down.shape, bf),
        ],
        in_specs=[vmem, vmem, vmem, hbm, hbm, hbm],
        out_specs=[vmem, hbm, hbm, hbm],
        scratch_shapes=[
            pltpu.VMEM((CHUNKS, 4, 4, 4, ROWS, QUARTER), bf),
            pltpu.VMEM((512, 1536), bf),
            pltpu.VMEM((2, 4096, 768), bf),
            pltpu.VMEM((2, 4, 384, TILE), bf),
            pltpu.VMEM((CHUNKS, 2, 4, 4, 16, QUARTER), bf),
            pltpu.VMEM((CHUNKS, 2, 4, 16, QUARTER), bf),
            pltpu.VMEM((CHUNKS, 2, 16, QUARTER), bf),
            pltpu.VMEM((CHUNKS, 2, 4, 4, ROWS, QUARTER), bf),
            pltpu.VMEM((CHUNKS, 2, 4, ROWS, QUARTER), bf),
            pltpu.VMEM((CHUNKS, 2, ROWS, QUARTER), bf),
            dma((CHUNKS,)),
            dma((2, 2)),
            dma((2, 2)),
            dma((5,)),
            dma((5,)),
            dma((CHUNKS, 3, 3, 4)),
            dma((CHUNKS, 3, 3, 4)),
            dma((CHUNKS, 3, 3, 4)),
            dma((CHUNKS, 3, 3, 4)),
        ],
        cost_estimate=pl.CostEstimate(
            flops=flops, bytes_accessed=150 << 20, transcendentals=2048 * 1536
        ),
        compiler_params=pltpu.CompilerParams(
            collective_id=0, has_side_effects=True, vmem_limit_bytes=60 << 20
        ),
    )(normed, merged, gates, w_gate, w_up, w_down)[0]


IMAGES = ("zx", "xz")


def image_kernel(
    text, image, meta, gain,
    merged, normed, gates,
    IMG, META, SQ, GB,
    im_send, im_recv, me_send, me_recv, sib_send, sib_recv, sq_send, sq_recv,
):
    me, core = place()
    barrier = pltpu.get_barrier_semaphore()
    neighbours = [device(moved(me, a, d), core) for a in "zx" for d in (1, -1)]
    neighbours += [device(moved(me, "y", d), core) for d in (1, 2, 3)]
    neighbours.append(device(me, 1 - core))
    for who in neighbours:
        pl.semaphore_signal(barrier, inc=1, device_id=who, device_id_type=MESH)
    pl.semaphore_wait(barrier, len(neighbours))
    z, x, y = me["z"], me["x"], me["y"]
    IMG[core, z, x] = image[...]
    META[core, z, x] = meta[...]

    def spot(full, at):
        return (core, *(slice(None) if a in full else at[a] for a in "zx"))

    def im_copy(p, k, j):
        axis, full = IMAGES[p][k], IMAGES[p][:k]
        way = 1 if j % 2 == 0 else -1
        at = me if j < 2 else moved(me, axis, -way)
        rows = pl.ds(0, 64) if j < 2 else pl.ds(32 * (j - 2), 32)
        part = IMG.at[(*spot(full, at), rows, pl.ds(512 * p, 512))]
        return pltpu.make_async_remote_copy(
            src_ref=part, dst_ref=part, send_sem=im_send.at[p, k, j], recv_sem=im_recv.at[p, k, j],
            device_id=device(moved(me, axis, way), core), device_id_type=MESH,
        )

    def me_copy(k, j):
        axis, full = IMAGES[0][k], IMAGES[0][:k]
        way = 1 if j % 2 == 0 else -1
        part = META.at[spot(full, me if j < 2 else moved(me, axis, -1))]
        return pltpu.make_async_remote_copy(
            src_ref=part, dst_ref=part, send_sem=me_send.at[k, j], recv_sem=me_recv.at[k, j],
            device_id=device(moved(me, axis, way), core), device_id_type=MESH,
        )

    def sibling(part, i, j):
        return pltpu.make_async_remote_copy(
            src_ref=part, dst_ref=part, send_sem=sib_send.at[i, j], recv_sem=sib_recv.at[i, j],
            device_id=device(me, 1 - core), device_id_type=MESH,
        )

    def sib_image(p, k, d):
        full = IMAGES[p][:k]
        at = moved(me, IMAGES[p][k], d)
        part = IMG.at[(*spot(full, at), slice(None), pl.ds(512 * p, 512))]
        return sibling(part, p, 3 * k + d)

    shared = []
    for p in range(2):
        shared.append(sib_image(p, 0, 0))
    for c in shared:
        c.start()
    for k in range(2):
        for j in (0, 1):
            me_copy(k, j).start()
            for p in range(2):
                im_copy(p, k, j).start()
        me_copy(k, 0).wait_recv()
        me_copy(k, 2).start()
        for j in (0, 1):
            for p in range(2):
                im_copy(p, k, j).wait_recv()
                im_copy(p, k, j + 2).start()
                shared.append(sib_image(p, k, 3 if j == 0 else 1))
                shared[-1].start()
        me_copy(k, 1).wait_recv()
        me_copy(k, 2).wait_recv()
        for p in range(2):
            for j in (2, 3):
                im_copy(p, k, j).wait_recv()
            shared.append(sib_image(p, k, 2))
            shared[-1].start()
    dest = sibling(META.at[core], 2, 0)
    dest.start()

    row = lax.broadcasted_iota(jnp.int32, (8, 1), 0)
    expert = 4 * (4 * z + x) + lax.rem(row + 2 * core, 4)
    expert = jnp.where(row < 4, expert, -1).astype(jnp.float32)
    for b in range(16):
        ids = META[core, b // 4, b % 4, pl.ds(0, 8), :]
        weights = META[core, b // 4, b % 4, pl.ds(8, 8), :]
        total = jnp.zeros((8, 128), jnp.float32)
        for i in range(8):
            total += jnp.where(ids[i:i + 1] == expert, weights[i:i + 1], 0.0)
        GB[pl.ds(8 * b, 8), :] = total
    gates[...] = jnp.transpose(GB[...])

    for c in shared:
        c.wait_recv()
    dest.wait_recv()
    lane = lax.broadcasted_iota(jnp.int32, (1, 128), 1)
    token = lax.broadcasted_iota(jnp.int32, (128, 128), 0) + 128 * ((z * 4 + x) * 2 + core)
    token = token.astype(jnp.float32)

    def group(g, carry):
        placed, present = carry
        c, gz = g // 4, lax.rem(g, 4)
        spots = [META[c, gz, i, pl.ds(16, 8), :][:1] for i in range(4)]
        hot = [
            (jnp.where(lane < 64, spots[i], spots[i + 1]) == token).astype(jnp.float32)
            for i in (0, 2)
        ]
        present += jnp.sum(hot[0] + hot[1], axis=1, keepdims=True)
        hot = jnp.concatenate(hot, axis=1).astype(jnp.bfloat16)
        placed += jnp.dot(
            hot, IMG[c, gz].reshape(256, QUARTER), preferred_element_type=jnp.float32
        )
        return placed, present

    placed, present = lax.fori_loop(
        0, 8, group, (jnp.zeros((128, QUARTER), jnp.float32), jnp.zeros((128, 1), jnp.float32))
    )
    whole = jnp.where(present > 0.5, placed, text[...].astype(jnp.float32))
    merged[...] = whole.astype(jnp.bfloat16)
    squares = jnp.sum(whole * whole, axis=1, keepdims=True)
    SQ[y] = jnp.broadcast_to(squares, (128, 128))
    sq = [
        pltpu.make_async_remote_copy(
            src_ref=SQ.at[y], dst_ref=SQ.at[y], send_sem=sq_send.at[d - 1], recv_sem=sq_recv.at[d - 1],
            device_id=device(moved(me, "y", d), core), device_id_type=MESH,
        )
        for d in (1, 2, 3)
    ]
    for c in sq:
        c.start()
    for c in sq:
        c.wait()
    mean = (SQ[0] + SQ[1] + SQ[2] + SQ[3])[:, :1] / 4096.0
    scale = lax.rsqrt(mean + 1e-06)
    normed[...] = (whole * scale * gain[pl.ds(y, 1), :]).astype(jnp.bfloat16)
    for k in range(2):
        for j in range(3):
            me_copy(k, j).wait_send()
        for p in range(2):
            for j in range(4):
                im_copy(p, k, j).wait_send()
    for c in shared:
        c.wait_send()
    dest.wait_send()


def merge(text, image, meta, gain):
    bf, f32 = jnp.bfloat16, jnp.float32
    vmem = pl.BlockSpec(memory_space=pltpu.VMEM)
    dma = pltpu.SemaphoreType.DMA
    return pl.pallas_call(
        image_kernel,
        out_shape=[
            jax.ShapeDtypeStruct(text.shape, bf),
            jax.ShapeDtypeStruct(text.shape, bf),
            jax.ShapeDtypeStruct((128, 128), f32),
        ],
        in_specs=[vmem] * 4,
        out_specs=[vmem] * 3,
        scratch_shapes=[
            pltpu.VMEM((2, 4, 4, 64, QUARTER), bf),
            pltpu.VMEM((2, 4, 4, 24, 128), f32),
            pltpu.VMEM((4, 128, 128), f32),
            pltpu.VMEM((128, 128), f32),
            dma((2, 2, 4)),
            dma((2, 2, 4)),
            dma((2, 3)),
            dma((2, 3)),
            dma((3, 7)),
            dma((3, 7)),
            dma((3,)),
            dma((3,)),
        ],
        cost_estimate=pl.CostEstimate(flops=1 << 29, bytes_accessed=6 << 20, transcendentals=128),
        compiler_params=pltpu.CompilerParams(
            collective_id=1, has_side_effects=True, vmem_limit_bytes=40 << 20
        ),
    )(text, image, meta, gain)


def on_device(
    text_rows, image_rows, image_dest, norm_gain, expert_ids, gate_weights, w_gate, w_up, w_down
):
    f32 = jnp.float32
    spots = image_dest.astype(f32)
    meta = jnp.concatenate(
        [
            expert_ids.astype(f32).T,
            gate_weights.T,
            jnp.broadcast_to(jnp.concatenate([spots, spots])[None], (8, 128)),
        ],
        axis=0,
    )
    merged, normed, gates = merge(text_rows, image_rows, meta, norm_gain.reshape(4, QUARTER))
    return experts(normed, merged, gates, w_gate, w_up, w_down)


def solution(mesh):
    placed = (
        P("seq", "exp"),
        P("seq", "exp"),
        P("seq"),
        P(),
        P("seq", None),
        P("seq", None),
        P("seq", None, "exp"),
        P("seq", None, "exp"),
        P("seq", "exp", None),
    )
    return jax.shard_map(
        on_device, mesh=mesh, in_specs=placed, out_specs=P("seq", "exp"), check_vma=False
    )
```

```python
import functools

import jax
import jax.numpy as jnp
from jax import lax
from jax.experimental import pallas as pl
from jax.experimental.pallas import tpu as pltpu
from jax.sharding import PartitionSpec as P

MESH = pl.DeviceIdType.MESH
CHUNKS = 4
ROWS = 32
QUARTER = 1024
DIMS = "yzx"
ORDERS = ("xyz", "yzx", "zxy")
WIDTHS = ((384, 384, 256), (384, 256, 384), (256, 384, 384), (384, 384, 256))
UNITS = 4
TILES = 8
TILE = 512


def place():
    s = lax.axis_index("seq")
    return {"z": s // 8, "x": (s // 2) % 4, "y": lax.axis_index("exp")}, s % 2


def device(at, core):
    return ((at["z"] * 4 + at["x"]) * 2 + core, at["y"])


def moved(at, axis, by):
    new = dict(at)
    new[axis] = (at[axis] + by + 4) % 4
    return new


def columns(q, p):
    return pl.ds(sum(WIDTHS[q][:p]), WIDTHS[q][p])


def expert_kernel(
    normed, merged, gates, w_gate, w_up, w_down,
    out, far_gate, far_up, far_down,
    X, H, WB, WD, half1, full1, full2, full3,
    own_sem, wb_sem, wd_sem, far_send, far_recv, ag_send, ag_recv, rs_send, rs_recv,
):
    me, core = place()
    barrier = pltpu.get_barrier_semaphore()
    neighbours = [device(moved(me, a, d), core) for a in "xyz" for d in (1, 2, 3)]
    neighbours.append(device(me, 1 - core))
    for who in neighbours:
        pl.semaphore_signal(barrier, inc=1, device_id=who, device_id_type=MESH)
    pl.semaphore_wait(barrier, len(neighbours))

    def slab(q, full, at, cols, rows=pl.ds(0, ROWS)):
        index = tuple(slice(None) if a in full else at[a] for a in DIMS)
        return (q, *index, rows, cols)

    far = [
        pltpu.make_async_remote_copy(
            src_ref=src, dst_ref=dst, send_sem=far_send.at[i], recv_sem=far_recv.at[i],
            device_id=device(me, 1 - core), device_id_type=MESH,
        )
        for i, (src, dst) in enumerate(
            (
                (w_gate.at[0], far_gate.at[0]),
                (w_up.at[0], far_up.at[0]),
                (w_gate.at[1], far_gate.at[1]),
                (w_up.at[1], far_up.at[1]),
                (w_down, far_down),
            )
        )
    ]
    own = [
        pltpu.make_async_copy(
            normed.at[pl.ds(ROWS * q, ROWS)], X.at[q, me["y"], me["z"], me["x"]], own_sem.at[q]
        )
        for q in range(CHUNKS)
    ]

    def ag_copy(q, p, k, j):
        order = ORDERS[p]
        axis, full = order[k], order[:k]
        cols = columns(q, p)
        by = (1, -1, 2)[j] if k < 2 else (1, -1, 1, -1)[j]
        if j < 2 or k < 2:
            index = slab(q, full, me, cols)
            src = normed.at[pl.ds(ROWS * q, ROWS), cols] if k == 0 else X.at[index]
        else:
            rows = pl.ds(0, 16) if j == 2 else pl.ds(16, 16)
            index = slab(q, full, moved(me, axis, -by), cols, rows)
            src = X.at[index]
        return pltpu.make_async_remote_copy(
            src_ref=src, dst_ref=X.at[index],
            send_sem=ag_send.at[q, p, k, j], recv_sem=ag_recv.at[q, p, k, j],
            device_id=device(moved(me, axis, by), core), device_id_type=MESH,
        )

    def ag_first(q, k):
        for p in range(3):
            if k:
                for j in range(3):
                    ag_copy(q, p, k - 1, j).wait_recv()
            for j in range(3 if k < 2 else 2):
                ag_copy(q, p, k, j).start()

    def ag_second(q):
        for p in range(3):
            for j in (0, 1):
                ag_copy(q, p, 2, j).wait_recv()
                ag_copy(q, p, 2, j + 2).start()

    def ag_end(q):
        for p in range(3):
            for j in (2, 3):
                ag_copy(q, p, 2, j).wait_recv()
            for k in range(3):
                for j in range(3 if k < 2 else 4):
                    ag_copy(q, p, k, j).wait_send()

    fulls = (full1, full2, full3)

    def rs_refs(q, p, k, j):
        order = ORDERS[p][::-1]
        axis, full = order[k], order[k + 1:]
        cols = columns(q, p)
        mid = (slice(None),) * len(full)
        by = (1, -1, 1, -1)[j] if k == 0 else (2, 1, -1)[j]
        if k == 0 and j < 2:
            rows = pl.ds(16 * j, 16)
            sent = slab(q, full, moved(me, axis, 2), cols, rows)
            kept = slab(q, full, moved(me, axis, by), cols, rows)
            got = half1.at[(q, j, *mid, slice(None), cols)]
        else:
            sent = slab(q, full, moved(me, axis, by), cols)
            kept = slab(q, full, me, cols)
            got = fulls[k].at[(q, j - 2 if k == 0 else j, *mid, slice(None), cols)]
        return sent, kept, got, device(moved(me, axis, by), core)

    def rs_copy(q, p, k, j):
        sent, _, got, who = rs_refs(q, p, k, j)
        return pltpu.make_async_remote_copy(
            src_ref=X.at[sent], dst_ref=got,
            send_sem=rs_send.at[q, p, k, j], recv_sem=rs_recv.at[q, p, k, j],
            device_id=who, device_id_type=MESH,
        )

    def f32(v):
        return v.astype(jnp.float32)

    def rs_first(q):
        for p in range(3):
            for j in (0, 1):
                rs_copy(q, p, 0, j).start()

    def rs_second(q):
        for p in range(3):
            for j in (0, 1):
                rs_copy(q, p, 0, j).wait_recv()
                _, kept, got, _ = rs_refs(q, p, 0, j)
                X[kept] = (f32(X[kept]) + f32(got[...])).astype(jnp.bfloat16)
                rs_copy(q, p, 0, j + 2).start()

    def rs_end(q, k):
        for p in range(3):
            last = (2, 3) if k == 0 else (0, 1, 2)
            kept = rs_refs(q, p, k, 2)[1]
            total = f32(X[kept])
            for j in last:
                rs_copy(q, p, k, j).wait_recv()
            for j in last:
                total += f32(rs_refs(q, p, k, j)[2][...])
            if k < 2:
                X[kept] = total.astype(jnp.bfloat16)
                for j in range(3):
                    rs_copy(q, p, k + 1, j).start()
            else:
                rows, cols = pl.ds(ROWS * q, ROWS), columns(q, p)
                out[rows, cols] = (total + f32(merged[rows, cols])).astype(jnp.bfloat16)

    def wb_copies(slot, gate, up, e):
        return [
            pltpu.make_async_copy(gate.at[e], WB.at[slot, :, pl.ds(0, 384)], wb_sem.at[slot, 0]),
            pltpu.make_async_copy(up.at[e], WB.at[slot, :, pl.ds(384, 384)], wb_sem.at[slot, 1]),
        ]

    def wb_start(e, slot):
        @pl.when(e < 2)
        def _():
            for c in wb_copies(slot, w_gate, w_up, e):
                c.start()

        @pl.when(e >= 2)
        def _():
            for c in wb_copies(slot, far_gate, far_up, e - 2):
                c.start()

    def wd_copies(n, slot):
        cols = pl.ds(pl.multiple_of(n * TILE, TILE), TILE)
        return [
            pltpu.make_async_copy(w_down.at[:, :, cols], WD.at[slot, pl.ds(0, 2)], wd_sem.at[slot, 0]),
            pltpu.make_async_copy(far_down.at[:, :, cols], WD.at[slot, pl.ds(2, 2)], wd_sem.at[slot, 1]),
        ]

    plan = {
        (0, 0): [lambda: ag_first(2, 1)],
        (0, 1): [lambda: ag_second(1), lambda: ag_first(2, 2)],
        (0, 2): [lambda: ag_first(3, 1)],
        (0, 4): [lambda: ag_end(1)],
        (0, 5): [lambda: ag_second(2), lambda: ag_first(3, 2)],
        (1, 1): [lambda: ag_second(3)],
        (1, 8): [lambda: ag_end(2)],
        (2, 8): [lambda: ag_end(3)],
    }

    def add(q, u, f, *args):
        plan.setdefault((q, u), []).append(lambda: f(*args))

    for q in range(CHUNKS):
        add(q, 11, rs_first, q)
        if q < CHUNKS - 1:
            add(q + 1, 1, rs_second, q)
            add(q + 1, 4, rs_end, q, 0)
            add(q + 1, 7, rs_end, q, 1)
            add(q + 1, 10, rs_end, q, 2)

    def hooks(q, u, units):
        for (pq, pu), actions in sorted(plan.items()):
            if pu in units:
                @pl.when((q == pq) & (u == pu))
                def _(actions=actions):
                    for act in actions:
                        act()

    for c in own:
        c.start()
    ag_first(0, 0)
    ag_first(1, 0)
    wb_start(0, 0)
    for c in own:
        c.wait()
    ag_first(0, 1)
    ag_first(1, 1)
    ag_first(0, 2)
    for c in far[:2]:
        c.start()
    for q in range(2, CHUNKS):
        ag_first(q, 0)
    for c in far[2:]:
        c.start()
    ag_second(0)
    ag_first(1, 2)
    ag_end(0)

    def chunk(q, carry):
        def unit(e, carry):
            slot = lax.rem(e, 2)

            for first, ready in ((1, far[:2]), (2, far[2:4]), (3, far[4:])):
                @pl.when((q == 0) & (e == first))
                def _(ready=ready):
                    for c in ready:
                        c.wait_recv()

            @pl.when((e < UNITS - 1) | (q < CHUNKS - 1))
            def _():
                wb_start(lax.rem(e + 1, UNITS), 1 - slot)

            @pl.when(e == UNITS - 1)
            def _():
                for c in wd_copies(0, 0):
                    c.start()

            for c in wb_copies(slot, w_gate, w_up, 0):
                c.wait()

            acc = jnp.zeros((512, 768), jnp.float32)
            for y in range(4):
                acc += jnp.dot(
                    X[q, y].reshape(512, QUARTER),
                    WB[slot, pl.ds(QUARTER * y, QUARTER), :],
                    preferred_element_type=jnp.float32,
                )
            g, u = acc[:, :384], acc[:, 384:]
            lane = lax.broadcasted_iota(jnp.int32, (16, ROWS, 128), 2)
            block = lax.broadcasted_iota(jnp.int32, (16, ROWS, 128), 0)
            rows = gates[pl.ds(pl.multiple_of(q * ROWS, ROWS), ROWS), :]
            weight = jnp.where(lane == 8 * block + e, rows[None], 0.0).reshape(512, 128)
            weight = jnp.sum(weight, axis=1, keepdims=True)
            hidden = g / (1.0 + jnp.exp(-g)) * u * weight
            H[:, pl.ds(pl.multiple_of(e * 384, 128), 384)] = hidden.astype(jnp.bfloat16)
            hooks(q, e, range(UNITS))
            return carry

        lax.fori_loop(0, UNITS, unit, 0)

        def tile(n, carry):
            slot = lax.rem(n, 2)

            @pl.when(n < TILES - 1)
            def _():
                for c in wd_copies(n + 1, 1 - slot):
                    c.start()

            for c in wd_copies(n, slot):
                c.wait()
            acc = jnp.dot(
                H[...], WD[slot].reshape(1536, TILE), preferred_element_type=jnp.float32
            )
            X[q, n // 2, :, :, :, pl.ds(pl.multiple_of(lax.rem(n, 2) * TILE, TILE), TILE)] = (
                acc.astype(jnp.bfloat16).reshape(4, 4, ROWS, TILE)
            )
            hooks(q, n + UNITS, range(UNITS, UNITS + TILES))
            return carry

        lax.fori_loop(0, TILES, tile, 0)
        return carry

    lax.fori_loop(0, CHUNKS, chunk, 0)
    last = CHUNKS - 1
    rs_second(last)
    for k in range(3):
        rs_end(last, k)
    for c in far:
        c.wait_send()
    for q in range(CHUNKS):
        for p in range(3):
            for k in range(3):
                for j in range(4 if k == 0 else 3):
                    rs_copy(q, p, k, j).wait_send()


def experts(normed, merged, gates, w_gate, w_up, w_down):
    bf = jnp.bfloat16
    hbm = pl.BlockSpec(memory_space=pl.ANY)
    vmem = pl.BlockSpec(memory_space=pltpu.VMEM)
    dma = pltpu.SemaphoreType.DMA
    flops = 2 * 2048 * 1536 * 4096 * 3
    return pl.pallas_call(
        expert_kernel,
        out_shape=[
            jax.ShapeDtypeStruct(merged.shape, bf),
            jax.ShapeDtypeStruct(w_gate.shape, bf),
            jax.ShapeDtypeStruct(w_up.shape, bf),
            jax.ShapeDtypeStruct(w_down.shape, bf),
        ],
        in_specs=[vmem, vmem, vmem, hbm, hbm, hbm],
        out_specs=[vmem, hbm, hbm, hbm],
        scratch_shapes=[
            pltpu.VMEM((CHUNKS, 4, 4, 4, ROWS, QUARTER), bf),
            pltpu.VMEM((512, 1536), bf),
            pltpu.VMEM((2, 4096, 768), bf),
            pltpu.VMEM((2, 4, 384, TILE), bf),
            pltpu.VMEM((CHUNKS, 2, 4, 4, 16, QUARTER), bf),
            pltpu.VMEM((CHUNKS, 2, 4, 4, ROWS, QUARTER), bf),
            pltpu.VMEM((CHUNKS, 3, 4, ROWS, QUARTER), bf),
            pltpu.VMEM((CHUNKS, 3, ROWS, QUARTER), bf),
            dma((CHUNKS,)),
            dma((2, 2)),
            dma((2, 2)),
            dma((5,)),
            dma((5,)),
            dma((CHUNKS, 3, 3, 4)),
            dma((CHUNKS, 3, 3, 4)),
            dma((CHUNKS, 3, 3, 4)),
            dma((CHUNKS, 3, 3, 4)),
        ],
        cost_estimate=pl.CostEstimate(
            flops=flops, bytes_accessed=150 << 20, transcendentals=2048 * 1536
        ),
        compiler_params=pltpu.CompilerParams(
            collective_id=0, has_side_effects=True, vmem_limit_bytes=60 << 20
        ),
    )(normed, merged, gates, w_gate, w_up, w_down)[0]


IMAGES = ("zx", "xz")


def image_kernel(
    text, image, meta, gain,
    merged, normed, gates,
    IMG, META, SQ, GB,
    im_send, im_recv, me_send, me_recv, sib_send, sib_recv, sq_send, sq_recv,
):
    me, core = place()
    barrier = pltpu.get_barrier_semaphore()
    neighbours = [device(moved(me, a, d), core) for a in "zx" for d in (1, -1)]
    neighbours += [device(moved(me, "y", d), core) for d in (1, 2, 3)]
    neighbours.append(device(me, 1 - core))
    for who in neighbours:
        pl.semaphore_signal(barrier, inc=1, device_id=who, device_id_type=MESH)
    pl.semaphore_wait(barrier, len(neighbours))
    z, x, y = me["z"], me["x"], me["y"]
    IMG[core, z, x] = image[...]
    META[core, z, x] = meta[...]

    def spot(full, at):
        return (core, *(slice(None) if a in full else at[a] for a in "zx"))

    def im_copy(p, k, j):
        axis, full = IMAGES[p][k], IMAGES[p][:k]
        way = 1 if j % 2 == 0 else -1
        at = me if j < 2 else moved(me, axis, -way)
        rows = pl.ds(0, 64) if j < 2 else pl.ds(32 * (j - 2), 32)
        part = IMG.at[(*spot(full, at), rows, pl.ds(512 * p, 512))]
        return pltpu.make_async_remote_copy(
            src_ref=part, dst_ref=part, send_sem=im_send.at[p, k, j], recv_sem=im_recv.at[p, k, j],
            device_id=device(moved(me, axis, way), core), device_id_type=MESH,
        )

    def me_copy(k, j):
        axis, full = IMAGES[0][k], IMAGES[0][:k]
        way = 1 if j % 2 == 0 else -1
        part = META.at[spot(full, me if j < 2 else moved(me, axis, -1))]
        return pltpu.make_async_remote_copy(
            src_ref=part, dst_ref=part, send_sem=me_send.at[k, j], recv_sem=me_recv.at[k, j],
            device_id=device(moved(me, axis, way), core), device_id_type=MESH,
        )

    def sibling(part, i, j):
        return pltpu.make_async_remote_copy(
            src_ref=part, dst_ref=part, send_sem=sib_send.at[i, j], recv_sem=sib_recv.at[i, j],
            device_id=device(me, 1 - core), device_id_type=MESH,
        )

    def sib_image(p, k, d):
        full = IMAGES[p][:k]
        at = moved(me, IMAGES[p][k], d)
        part = IMG.at[(*spot(full, at), slice(None), pl.ds(512 * p, 512))]
        return sibling(part, p, 3 * k + d)

    shared = []
    for p in range(2):
        shared.append(sib_image(p, 0, 0))
    for c in shared:
        c.start()
    for k in range(2):
        for j in (0, 1):
            me_copy(k, j).start()
            for p in range(2):
                im_copy(p, k, j).start()
        me_copy(k, 0).wait_recv()
        me_copy(k, 2).start()
        for j in (0, 1):
            for p in range(2):
                im_copy(p, k, j).wait_recv()
                im_copy(p, k, j + 2).start()
                shared.append(sib_image(p, k, 3 if j == 0 else 1))
                shared[-1].start()
        me_copy(k, 1).wait_recv()
        me_copy(k, 2).wait_recv()
        for p in range(2):
            for j in (2, 3):
                im_copy(p, k, j).wait_recv()
            shared.append(sib_image(p, k, 2))
            shared[-1].start()
    dest = sibling(META.at[core], 2, 0)
    dest.start()

    row = lax.broadcasted_iota(jnp.int32, (8, 1), 0)
    expert = 4 * (4 * z + x) + lax.rem(row + 2 * core, 4)
    expert = jnp.where(row < 4, expert, -1).astype(jnp.float32)
    for b in range(16):
        ids = META[core, b // 4, b % 4, pl.ds(0, 8), :]
        weights = META[core, b // 4, b % 4, pl.ds(8, 8), :]
        total = jnp.zeros((8, 128), jnp.float32)
        for i in range(8):
            total += jnp.where(ids[i:i + 1] == expert, weights[i:i + 1], 0.0)
        GB[pl.ds(8 * b, 8), :] = total
    gates[...] = jnp.transpose(GB[...])

    for c in shared:
        c.wait_recv()
    dest.wait_recv()
    lane = lax.broadcasted_iota(jnp.int32, (1, 128), 1)
    token = lax.broadcasted_iota(jnp.int32, (128, 128), 0) + 128 * ((z * 4 + x) * 2 + core)
    token = token.astype(jnp.float32)

    def group(g, carry):
        placed, present = carry
        c, gz = g // 4, lax.rem(g, 4)
        spots = [META[c, gz, i, pl.ds(16, 8), :][:1] for i in range(4)]
        hot = [
            (jnp.where(lane < 64, spots[i], spots[i + 1]) == token).astype(jnp.float32)
            for i in (0, 2)
        ]
        present += jnp.sum(hot[0] + hot[1], axis=1, keepdims=True)
        hot = jnp.concatenate(hot, axis=1).astype(jnp.bfloat16)
        placed += jnp.dot(
            hot, IMG[c, gz].reshape(256, QUARTER), preferred_element_type=jnp.float32
        )
        return placed, present

    placed, present = lax.fori_loop(
        0, 8, group, (jnp.zeros((128, QUARTER), jnp.float32), jnp.zeros((128, 1), jnp.float32))
    )
    whole = jnp.where(present > 0.5, placed, text[...].astype(jnp.float32))
    merged[...] = whole.astype(jnp.bfloat16)
    squares = jnp.sum(whole * whole, axis=1, keepdims=True)
    SQ[y] = jnp.broadcast_to(squares, (128, 128))
    sq = [
        pltpu.make_async_remote_copy(
            src_ref=SQ.at[y], dst_ref=SQ.at[y], send_sem=sq_send.at[d - 1], recv_sem=sq_recv.at[d - 1],
            device_id=device(moved(me, "y", d), core), device_id_type=MESH,
        )
        for d in (1, 2, 3)
    ]
    for c in sq:
        c.start()
    for c in sq:
        c.wait()
    mean = (SQ[0] + SQ[1] + SQ[2] + SQ[3])[:, :1] / 4096.0
    scale = lax.rsqrt(mean + 1e-06)
    normed[...] = (whole * scale * gain[pl.ds(y, 1), :]).astype(jnp.bfloat16)
    for k in range(2):
        for j in range(3):
            me_copy(k, j).wait_send()
        for p in range(2):
            for j in range(4):
                im_copy(p, k, j).wait_send()
    for c in shared:
        c.wait_send()
    dest.wait_send()


def merge(text, image, meta, gain):
    bf, f32 = jnp.bfloat16, jnp.float32
    vmem = pl.BlockSpec(memory_space=pltpu.VMEM)
    dma = pltpu.SemaphoreType.DMA
    return pl.pallas_call(
        image_kernel,
        out_shape=[
            jax.ShapeDtypeStruct(text.shape, bf),
            jax.ShapeDtypeStruct(text.shape, bf),
            jax.ShapeDtypeStruct((128, 128), f32),
        ],
        in_specs=[vmem] * 4,
        out_specs=[vmem] * 3,
        scratch_shapes=[
            pltpu.VMEM((2, 4, 4, 64, QUARTER), bf),
            pltpu.VMEM((2, 4, 4, 24, 128), f32),
            pltpu.VMEM((4, 128, 128), f32),
            pltpu.VMEM((128, 128), f32),
            dma((2, 2, 4)),
            dma((2, 2, 4)),
            dma((2, 3)),
            dma((2, 3)),
            dma((3, 7)),
            dma((3, 7)),
            dma((3,)),
            dma((3,)),
        ],
        cost_estimate=pl.CostEstimate(flops=1 << 29, bytes_accessed=6 << 20, transcendentals=128),
        compiler_params=pltpu.CompilerParams(
            collective_id=1, has_side_effects=True, vmem_limit_bytes=40 << 20
        ),
    )(text, image, meta, gain)


def on_device(
    text_rows, image_rows, image_dest, norm_gain, expert_ids, gate_weights, w_gate, w_up, w_down
):
    f32 = jnp.float32
    spots = image_dest.astype(f32)
    meta = jnp.concatenate(
        [
            expert_ids.astype(f32).T,
            gate_weights.T,
            jnp.broadcast_to(jnp.concatenate([spots, spots])[None], (8, 128)),
        ],
        axis=0,
    )
    merged, normed, gates = merge(text_rows, image_rows, meta, norm_gain.reshape(4, QUARTER))
    return experts(normed, merged, gates, w_gate, w_up, w_down)


def solution(mesh):
    placed = (
        P("seq", "exp"),
        P("seq", "exp"),
        P("seq"),
        P(),
        P("seq", None),
        P("seq", None),
        P("seq", None, "exp"),
        P("seq", None, "exp"),
        P("seq", "exp", None),
    )
    return jax.shard_map(
        on_device, mesh=mesh, in_specs=placed, out_specs=P("seq", "exp"), check_vma=False
    )
```

```python
import functools

import jax
import jax.numpy as jnp
from jax import lax
from jax.experimental import pallas as pl
from jax.experimental.pallas import tpu as pltpu
from jax.sharding import PartitionSpec as P

MESH = pl.DeviceIdType.MESH
CHUNKS = 4
ROWS = 32
QUARTER = 1024
DIMS = "yzx"
ORDERS = ("xyz", "yzx", "zxy")
WIDTHS = ((384, 384, 256), (384, 256, 384), (256, 384, 384), (384, 384, 256))
UNITS = 4
TILES = 8
TILE = 512


def place():
    s = lax.axis_index("seq")
    return {"z": s // 8, "x": (s // 2) % 4, "y": lax.axis_index("exp")}, s % 2


def device(at, core):
    return ((at["z"] * 4 + at["x"]) * 2 + core, at["y"])


def moved(at, axis, by):
    new = dict(at)
    new[axis] = (at[axis] + by + 4) % 4
    return new


def columns(q, p):
    return pl.ds(sum(WIDTHS[q][:p]), WIDTHS[q][p])


def expert_kernel(
    normed, merged, gates, w_gate, w_up, w_down,
    out, far_gate, far_up, far_down,
    X, H, WB, WD, half1, full1, full2, full3,
    own_sem, wb_sem, wd_sem, far_send, far_recv, ag_send, ag_recv, rs_send, rs_recv,
):
    me, core = place()
    barrier = pltpu.get_barrier_semaphore()
    neighbours = [device(moved(me, a, d), core) for a in "xyz" for d in (1, 2, 3)]
    neighbours.append(device(me, 1 - core))
    for who in neighbours:
        pl.semaphore_signal(barrier, inc=1, device_id=who, device_id_type=MESH)
    pl.semaphore_wait(barrier, len(neighbours))

    def slab(q, full, at, cols, rows=pl.ds(0, ROWS)):
        index = tuple(slice(None) if a in full else at[a] for a in DIMS)
        return (q, *index, rows, cols)

    far = [
        pltpu.make_async_remote_copy(
            src_ref=src, dst_ref=dst, send_sem=far_send.at[i], recv_sem=far_recv.at[i],
            device_id=device(me, 1 - core), device_id_type=MESH,
        )
        for i, (src, dst) in enumerate(
            (
                (w_gate.at[0], far_gate.at[0]),
                (w_up.at[0], far_up.at[0]),
                (w_gate.at[1], far_gate.at[1]),
                (w_up.at[1], far_up.at[1]),
                (w_down, far_down),
            )
        )
    ]
    own = [
        pltpu.make_async_copy(
            normed.at[pl.ds(ROWS * q, ROWS)], X.at[q, me["y"], me["z"], me["x"]], own_sem.at[q]
        )
        for q in range(CHUNKS)
    ]

    def ag_copy(q, p, k, j):
        order = ORDERS[p]
        axis, full = order[k], order[:k]
        cols = columns(q, p)
        by = (1, -1, 2)[j] if k < 2 else (1, -1, 1, -1)[j]
        if j < 2 or k < 2:
            index = slab(q, full, me, cols)
            src = normed.at[pl.ds(ROWS * q, ROWS), cols] if k == 0 else X.at[index]
        else:
            rows = pl.ds(0, 16) if j == 2 else pl.ds(16, 16)
            index = slab(q, full, moved(me, axis, -by), cols, rows)
            src = X.at[index]
        return pltpu.make_async_remote_copy(
            src_ref=src, dst_ref=X.at[index],
            send_sem=ag_send.at[q, p, k, j], recv_sem=ag_recv.at[q, p, k, j],
            device_id=device(moved(me, axis, by), core), device_id_type=MESH,
        )

    def ag_first(q, k):
        for p in range(3):
            if k:
                for j in range(3):
                    ag_copy(q, p, k - 1, j).wait_recv()
            for j in range(3 if k < 2 else 2):
                ag_copy(q, p, k, j).start()

    def ag_second(q):
        for p in range(3):
            for j in (0, 1):
                ag_copy(q, p, 2, j).wait_recv()
                ag_copy(q, p, 2, j + 2).start()

    def ag_end(q):
        for p in range(3):
            for j in (2, 3):
                ag_copy(q, p, 2, j).wait_recv()
            for k in range(3):
                for j in range(3 if k < 2 else 4):
                    ag_copy(q, p, k, j).wait_send()

    fulls = (full1, full2, full3)

    def rs_refs(q, p, k, j):
        order = ORDERS[p][::-1]
        axis, full = order[k], order[k + 1:]
        cols = columns(q, p)
        mid = (slice(None),) * len(full)
        by = (1, -1, 1, -1)[j] if k == 0 else (2, 1, -1)[j]
        if k == 0 and j < 2:
            rows = pl.ds(16 * j, 16)
            sent = slab(q, full, moved(me, axis, 2), cols, rows)
            kept = slab(q, full, moved(me, axis, by), cols, rows)
            got = half1.at[(q, j, *mid, slice(None), cols)]
        else:
            sent = slab(q, full, moved(me, axis, by), cols)
            kept = slab(q, full, me, cols)
            got = fulls[k].at[(q, j - 2 if k == 0 else j, *mid, slice(None), cols)]
        return sent, kept, got, device(moved(me, axis, by), core)

    def rs_copy(q, p, k, j):
        sent, _, got, who = rs_refs(q, p, k, j)
        return pltpu.make_async_remote_copy(
            src_ref=X.at[sent], dst_ref=got,
            send_sem=rs_send.at[q, p, k, j], recv_sem=rs_recv.at[q, p, k, j],
            device_id=who, device_id_type=MESH,
        )

    def f32(v):
        return v.astype(jnp.float32)

    def rs_first(q):
        for p in range(3):
            for j in (0, 1):
                rs_copy(q, p, 0, j).start()

    def rs_second(q):
        for p in range(3):
            for j in (0, 1):
                rs_copy(q, p, 0, j).wait_recv()
                _, kept, got, _ = rs_refs(q, p, 0, j)
                X[kept] = (f32(X[kept]) + f32(got[...])).astype(jnp.bfloat16)
                rs_copy(q, p, 0, j + 2).start()

    def rs_end(q, k):
        for p in range(3):
            last = (2, 3) if k == 0 else (0, 1, 2)
            kept = rs_refs(q, p, k, 2)[1]
            total = f32(X[kept])
            for j in last:
                rs_copy(q, p, k, j).wait_recv()
            for j in last:
                total += f32(rs_refs(q, p, k, j)[2][...])
            if k < 2:
                X[kept] = total.astype(jnp.bfloat16)
                for j in range(3):
                    rs_copy(q, p, k + 1, j).start()
            else:
                rows, cols = pl.ds(ROWS * q, ROWS), columns(q, p)
                out[rows, cols] = (total + f32(merged[rows, cols])).astype(jnp.bfloat16)

    def wb_copies(slot, gate, up, e):
        return [
            pltpu.make_async_copy(gate.at[e], WB.at[slot, :, pl.ds(0, 384)], wb_sem.at[slot, 0]),
            pltpu.make_async_copy(up.at[e], WB.at[slot, :, pl.ds(384, 384)], wb_sem.at[slot, 1]),
        ]

    def wb_start(e, slot):
        @pl.when(e < 2)
        def _():
            for c in wb_copies(slot, w_gate, w_up, e):
                c.start()

        @pl.when(e >= 2)
        def _():
            for c in wb_copies(slot, far_gate, far_up, e - 2):
                c.start()

    def wd_copies(n, slot):
        cols = pl.ds(pl.multiple_of(n * TILE, TILE), TILE)
        return [
            pltpu.make_async_copy(w_down.at[:, :, cols], WD.at[slot, pl.ds(0, 2)], wd_sem.at[slot, 0]),
            pltpu.make_async_copy(far_down.at[:, :, cols], WD.at[slot, pl.ds(2, 2)], wd_sem.at[slot, 1]),
        ]

    plan = {
        (0, 0): [lambda: ag_first(2, 1)],
        (0, 1): [lambda: ag_second(1), lambda: ag_first(2, 2)],
        (0, 2): [lambda: ag_first(3, 1)],
        (0, 4): [lambda: ag_end(1)],
        (0, 5): [lambda: ag_second(2), lambda: ag_first(3, 2)],
        (1, 1): [lambda: ag_second(3)],
        (1, 8): [lambda: ag_end(2)],
        (2, 8): [lambda: ag_end(3)],
    }

    def add(q, u, f, *args):
        plan.setdefault((q, u), []).append(lambda: f(*args))

    for q in range(CHUNKS):
        add(q, 11, rs_first, q)
        if q < CHUNKS - 1:
            add(q + 1, 1, rs_second, q)
            add(q + 1, 4, rs_end, q, 0)
            add(q + 1, 7, rs_end, q, 1)
            add(q + 1, 10, rs_end, q, 2)

    def hooks(q, u, units):
        for (pq, pu), actions in sorted(plan.items()):
            if pu in units:
                @pl.when((q == pq) & (u == pu))
                def _(actions=actions):
                    for act in actions:
                        act()

    for c in own:
        c.start()
    ag_first(0, 0)
    ag_first(1, 0)
    wb_start(0, 0)
    for c in own:
        c.wait()
    ag_first(0, 1)
    ag_first(1, 1)
    ag_first(0, 2)
    for c in far[:2]:
        c.start()
    for q in range(2, CHUNKS):
        ag_first(q, 0)
    for c in far[2:]:
        c.start()
    ag_second(0)
    ag_first(1, 2)
    ag_end(0)

    def chunk(q, carry):
        def unit(e, carry):
            slot = lax.rem(e, 2)

            for first, ready in ((1, far[:2]), (2, far[2:4]), (3, far[4:])):
                @pl.when((q == 0) & (e == first))
                def _(ready=ready):
                    for c in ready:
                        c.wait_recv()

            @pl.when((e < UNITS - 1) | (q < CHUNKS - 1))
            def _():
                wb_start(lax.rem(e + 1, UNITS), 1 - slot)

            @pl.when(e == UNITS - 1)
            def _():
                for c in wd_copies(0, 0):
                    c.start()

            for c in wb_copies(slot, w_gate, w_up, 0):
                c.wait()

            acc = jnp.zeros((512, 768), jnp.float32)
            for y in range(4):
                acc += jnp.dot(
                    X[q, y].reshape(512, QUARTER),
                    WB[slot, pl.ds(QUARTER * y, QUARTER), :],
                    preferred_element_type=jnp.float32,
                )
            g, u = acc[:, :384], acc[:, 384:]
            lane = lax.broadcasted_iota(jnp.int32, (16, ROWS, 128), 2)
            block = lax.broadcasted_iota(jnp.int32, (16, ROWS, 128), 0)
            rows = gates[pl.ds(pl.multiple_of(q * ROWS, ROWS), ROWS), :]
            weight = jnp.where(lane == 8 * block + e, rows[None], 0.0).reshape(512, 128)
            weight = jnp.sum(weight, axis=1, keepdims=True)
            hidden = g / (1.0 + jnp.exp(-g)) * u * weight
            H[:, pl.ds(pl.multiple_of(e * 384, 128), 384)] = hidden.astype(jnp.bfloat16)
            hooks(q, e, range(UNITS))
            return carry

        lax.fori_loop(0, UNITS, unit, 0)

        def tile(n, carry):
            slot = lax.rem(n, 2)

            @pl.when(n < TILES - 1)
            def _():
                for c in wd_copies(n + 1, 1 - slot):
                    c.start()

            for c in wd_copies(n, slot):
                c.wait()
            acc = jnp.dot(
                H[...], WD[slot].reshape(1536, TILE), preferred_element_type=jnp.float32
            )
            X[q, n // 2, :, :, :, pl.ds(pl.multiple_of(lax.rem(n, 2) * TILE, TILE), TILE)] = (
                acc.astype(jnp.bfloat16).reshape(4, 4, ROWS, TILE)
            )
            hooks(q, n + UNITS, range(UNITS, UNITS + TILES))
            return carry

        lax.fori_loop(0, TILES, tile, 0)
        return carry

    lax.fori_loop(0, CHUNKS, chunk, 0)
    last = CHUNKS - 1
    rs_second(last)
    for k in range(3):
        rs_end(last, k)
    for c in far:
        c.wait_send()
    for q in range(CHUNKS):
        for p in range(3):
            for k in range(3):
                for j in range(4 if k == 0 else 3):
                    rs_copy(q, p, k, j).wait_send()


def experts(normed, merged, gates, w_gate, w_up, w_down):
    bf = jnp.bfloat16
    hbm = pl.BlockSpec(memory_space=pl.ANY)
    vmem = pl.BlockSpec(memory_space=pltpu.VMEM)
    dma = pltpu.SemaphoreType.DMA
    flops = 2 * 2048 * 1536 * 4096 * 3
    return pl.pallas_call(
        expert_kernel,
        out_shape=[
            jax.ShapeDtypeStruct(merged.shape, bf),
            jax.ShapeDtypeStruct(w_gate.shape, bf),
            jax.ShapeDtypeStruct(w_up.shape, bf),
            jax.ShapeDtypeStruct(w_down.shape, bf),
        ],
        in_specs=[vmem, vmem, vmem, hbm, hbm, hbm],
        out_specs=[vmem, hbm, hbm, hbm],
        scratch_shapes=[
            pltpu.VMEM((CHUNKS, 4, 4, 4, ROWS, QUARTER), bf),
            pltpu.VMEM((512, 1536), bf),
            pltpu.VMEM((2, 4096, 768), bf),
            pltpu.VMEM((2, 4, 384, TILE), bf),
            pltpu.VMEM((CHUNKS, 2, 4, 4, 16, QUARTER), bf),
            pltpu.VMEM((CHUNKS, 2, 4, 4, ROWS, QUARTER), bf),
            pltpu.VMEM((CHUNKS, 3, 4, ROWS, QUARTER), bf),
            pltpu.VMEM((CHUNKS, 3, ROWS, QUARTER), bf),
            dma((CHUNKS,)),
            dma((2, 2)),
            dma((2, 2)),
            dma((5,)),
            dma((5,)),
            dma((CHUNKS, 3, 3, 4)),
            dma((CHUNKS, 3, 3, 4)),
            dma((CHUNKS, 3, 3, 4)),
            dma((CHUNKS, 3, 3, 4)),
        ],
        cost_estimate=pl.CostEstimate(
            flops=flops, bytes_accessed=150 << 20, transcendentals=2048 * 1536
        ),
        compiler_params=pltpu.CompilerParams(
            collective_id=0, has_side_effects=True, vmem_limit_bytes=60 << 20
        ),
    )(normed, merged, gates, w_gate, w_up, w_down)[0]


IMAGES = ("zx", "xz")


def image_kernel(
    text, image, meta, gain,
    merged, normed, gates,
    IMG, META, SQ, GB,
    im_send, im_recv, me_send, me_recv, sib_send, sib_recv, sq_send, sq_recv,
):
    me, core = place()
    barrier = pltpu.get_barrier_semaphore()
    neighbours = [device(moved(me, a, d), core) for a in "zx" for d in (1, 2, 3)]
    neighbours += [device(moved(me, "y", d), core) for d in (1, 2, 3)]
    neighbours.append(device(me, 1 - core))
    for who in neighbours:
        pl.semaphore_signal(barrier, inc=1, device_id=who, device_id_type=MESH)
    pl.semaphore_wait(barrier, len(neighbours))
    z, x, y = me["z"], me["x"], me["y"]
    IMG[core, z, x] = image[...]
    META[core, z, x] = meta[...]

    def spot(full, at):
        return (core, *(slice(None) if a in full else at[a] for a in "zx"))

    def im_copy(p, k, j):
        axis, full = IMAGES[p][k], IMAGES[p][:k]
        way = (1, -1, 2)[j] if k == 0 else (1, -1, 1, -1)[j]
        whole = k == 0 or j < 2
        at = me if whole else moved(me, axis, -way)
        rows = pl.ds(0, 64) if whole else pl.ds(32 * (j - 2), 32)
        part = IMG.at[(*spot(full, at), rows, pl.ds(512 * p, 512))]
        return pltpu.make_async_remote_copy(
            src_ref=part, dst_ref=part, send_sem=im_send.at[p, k, j], recv_sem=im_recv.at[p, k, j],
            device_id=device(moved(me, axis, way), core), device_id_type=MESH,
        )

    def me_copy(k, j):
        axis, full = IMAGES[0][k], IMAGES[0][:k]
        way = (1, -1, 2)[j]
        part = META.at[spot(full, me)]
        return pltpu.make_async_remote_copy(
            src_ref=part, dst_ref=part, send_sem=me_send.at[k, j], recv_sem=me_recv.at[k, j],
            device_id=device(moved(me, axis, way), core), device_id_type=MESH,
        )

    def sibling(part, i, j):
        return pltpu.make_async_remote_copy(
            src_ref=part, dst_ref=part, send_sem=sib_send.at[i, j], recv_sem=sib_recv.at[i, j],
            device_id=device(me, 1 - core), device_id_type=MESH,
        )

    def sib_image(p, k, d):
        full = IMAGES[p][:k]
        at = moved(me, IMAGES[p][k], d)
        part = IMG.at[(*spot(full, at), slice(None), pl.ds(512 * p, 512))]
        return sibling(part, p, 3 * k + d)

    shared = []
    for p in range(2):
        shared.append(sib_image(p, 0, 0))
    for c in shared:
        c.start()
    for k in range(2):
        for j in range(3):
            me_copy(k, j).start()
            if j < 2 or k == 0:
                for p in range(2):
                    im_copy(p, k, j).start()
        for j in (0, 1):
            for p in range(2):
                im_copy(p, k, j).wait_recv()
                if k:
                    im_copy(p, k, j + 2).start()
                shared.append(sib_image(p, k, 3 if j == 0 else 1))
                shared[-1].start()
        for j in range(3):
            me_copy(k, j).wait_recv()
        for p in range(2):
            for j in (2, 3) if k else (2,):
                im_copy(p, k, j).wait_recv()
            shared.append(sib_image(p, k, 2))
            shared[-1].start()
    dest = sibling(META.at[core], 2, 0)
    dest.start()

    row = lax.broadcasted_iota(jnp.int32, (8, 1), 0)
    expert = 4 * (4 * z + x) + lax.rem(row + 2 * core, 4)
    expert = jnp.where(row < 4, expert, -1).astype(jnp.float32)
    for b in range(16):
        ids = META[core, b // 4, b % 4, pl.ds(0, 8), :]
        weights = META[core, b // 4, b % 4, pl.ds(8, 8), :]
        total = jnp.zeros((8, 128), jnp.float32)
        for i in range(8):
            total += jnp.where(ids[i:i + 1] == expert, weights[i:i + 1], 0.0)
        GB[pl.ds(8 * b, 8), :] = total
    gates[...] = jnp.transpose(GB[...])

    for c in shared:
        c.wait_recv()
    dest.wait_recv()
    lane = lax.broadcasted_iota(jnp.int32, (1, 128), 1)
    token = lax.broadcasted_iota(jnp.int32, (128, 128), 0) + 128 * ((z * 4 + x) * 2 + core)
    token = token.astype(jnp.float32)

    def group(g, carry):
        placed, present = carry
        c, gz = g // 4, lax.rem(g, 4)
        spots = [META[c, gz, i, pl.ds(16, 8), :][:1] for i in range(4)]
        hot = [
            (jnp.where(lane < 64, spots[i], spots[i + 1]) == token).astype(jnp.float32)
            for i in (0, 2)
        ]
        present += jnp.sum(hot[0] + hot[1], axis=1, keepdims=True)
        hot = jnp.concatenate(hot, axis=1).astype(jnp.bfloat16)
        placed += jnp.dot(
            hot, IMG[c, gz].reshape(256, QUARTER), preferred_element_type=jnp.float32
        )
        return placed, present

    placed, present = lax.fori_loop(
        0, 8, group, (jnp.zeros((128, QUARTER), jnp.float32), jnp.zeros((128, 1), jnp.float32))
    )
    whole = jnp.where(present > 0.5, placed, text[...].astype(jnp.float32))
    merged[...] = whole.astype(jnp.bfloat16)
    squares = jnp.sum(whole * whole, axis=1, keepdims=True)
    SQ[y] = jnp.broadcast_to(squares, (128, 128))
    sq = [
        pltpu.make_async_remote_copy(
            src_ref=SQ.at[y], dst_ref=SQ.at[y], send_sem=sq_send.at[d - 1], recv_sem=sq_recv.at[d - 1],
            device_id=device(moved(me, "y", d), core), device_id_type=MESH,
        )
        for d in (1, 2, 3)
    ]
    for c in sq:
        c.start()
    for c in sq:
        c.wait()
    mean = (SQ[0] + SQ[1] + SQ[2] + SQ[3])[:, :1] / 4096.0
    scale = lax.rsqrt(mean + 1e-06)
    normed[...] = (whole * scale * gain[pl.ds(y, 1), :]).astype(jnp.bfloat16)
    for k in range(2):
        for j in range(3):
            me_copy(k, j).wait_send()
        for p in range(2):
            for j in range(4 if k else 3):
                im_copy(p, k, j).wait_send()
    for c in shared:
        c.wait_send()
    dest.wait_send()


def merge(text, image, meta, gain):
    bf, f32 = jnp.bfloat16, jnp.float32
    vmem = pl.BlockSpec(memory_space=pltpu.VMEM)
    dma = pltpu.SemaphoreType.DMA
    return pl.pallas_call(
        image_kernel,
        out_shape=[
            jax.ShapeDtypeStruct(text.shape, bf),
            jax.ShapeDtypeStruct(text.shape, bf),
            jax.ShapeDtypeStruct((128, 128), f32),
        ],
        in_specs=[vmem] * 4,
        out_specs=[vmem] * 3,
        scratch_shapes=[
            pltpu.VMEM((2, 4, 4, 64, QUARTER), bf),
            pltpu.VMEM((2, 4, 4, 24, 128), f32),
            pltpu.VMEM((4, 128, 128), f32),
            pltpu.VMEM((128, 128), f32),
            dma((2, 2, 4)),
            dma((2, 2, 4)),
            dma((2, 3)),
            dma((2, 3)),
            dma((3, 7)),
            dma((3, 7)),
            dma((3,)),
            dma((3,)),
        ],
        cost_estimate=pl.CostEstimate(flops=1 << 29, bytes_accessed=6 << 20, transcendentals=128),
        compiler_params=pltpu.CompilerParams(
            collective_id=1, has_side_effects=True, vmem_limit_bytes=40 << 20
        ),
    )(text, image, meta, gain)


def on_device(
    text_rows, image_rows, image_dest, norm_gain, expert_ids, gate_weights, w_gate, w_up, w_down
):
    f32 = jnp.float32
    spots = image_dest.astype(f32)
    meta = jnp.concatenate(
        [
            expert_ids.astype(f32).T,
            gate_weights.T,
            jnp.broadcast_to(jnp.concatenate([spots, spots])[None], (8, 128)),
        ],
        axis=0,
    )
    merged, normed, gates = merge(text_rows, image_rows, meta, norm_gain.reshape(4, QUARTER))
    return experts(normed, merged, gates, w_gate, w_up, w_down)


def solution(mesh):
    placed = (
        P("seq", "exp"),
        P("seq", "exp"),
        P("seq"),
        P(),
        P("seq", None),
        P("seq", None),
        P("seq", None, "exp"),
        P("seq", None, "exp"),
        P("seq", "exp", None),
    )
    return jax.shard_map(
        on_device, mesh=mesh, in_specs=placed, out_specs=P("seq", "exp"), check_vma=False
    )
```
